32 devices in a mesh: groups: 2 (over x), row: 16 (over z, y, core).
Axes of the slice: x: 2, y: 2, z: 4, core: 2. Of those that a mesh axis runs over, the one named last changes fastest.
Arguments:
- homolog_embedding: bfloat16 [512, 128, 64], P('groups', 'row'), parts along dimension 0, may hold values from -6 to 6
- coupling_embedding: bfloat16 [256, 128, 128], P(('groups', 'row')), parts along dimension 0, may hold values from -4.2 to 4.2
- entry_indicator: int32 [512, 128], P('groups', 'row'), parts along dimension 0, may hold values 0 or 1
- nonpadding_indicator: int32 [256], P(('groups', 'row')), parts along dimension 0, may hold values 0 or 1
- first_factor_matrix: bfloat16 [64, 32], replicated, may hold values from -0.75 to 0.75
- second_factor_matrix: bfloat16 [64, 32], replicated, may hold values from -0.75 to 0.75
- tensor_product_matrix: bfloat16 [1024, 128], replicated, may hold values from -1.5 to 1.5
- coupling_to_groups: bfloat16 [128, 8], replicated, may hold values from -15 to 15
- query_key_gate_matrix: bfloat16 [64, 1024], replicated, may hold values from -0.75 to 0.75
- attention_final_matrix: bfloat16 [256, 64], replicated, may hold values from -0.375 to 0.375
Outputs:
- pair_output: bfloat16 [256, 128, 128], P(('groups', 'row')), parts along dimension 0
- refreshed_homologs: bfloat16 [512, 128, 64], P('groups', 'row'), parts along dimension 0
The draws below stay inside these ranges and needn't reach their ends.
There are 2 independent parts, one for each index of `groups`. The reference program is written for one: setup_inputs(seed, part) draws one part's arguments, and reference() takes and returns one part's arrays. A program takes and returns all parts, laid end to end along the dimension named above; an argument that names none is the same for every part. Nothing has to cross between parts.
All inputs are finite; a program needn't handle non-finite values. No bound on the sum of `entry_indicator` or of `nonpadding_indicator` on one device may be relied on, other than what follows from the above.
Results may differ from the reference program's by a relative error of at most 0.019.
The reference program's roundings to bfloat16 on the way count: a program that leaves them out, or rounds other values in their place, can miss the bound.
Values may be sent and summed in bfloat16 or wider, within the bound.
A program may use at most 128 MiB of HBM per device.

```python
import math
import jax
import jax.numpy as jnp
from jax import lax

FEATURE_DEPTH = 64
CZ = 128
FACTOR_WIDE = 32
ATTN_GROUPS = 8
ATTN_DIM = 32
TOK_DEV = 8
HOMOLOG_NUMBER = 256
CHAIN_LENGTH = 128


def shared_columns(key):
    return jnp.clip(jax.random.normal(key, (CZ, ATTN_GROUPS), jnp.float32), -4.0, 4.0)


def draw_coupling_embedding(key, part):
    key = jax.random.fold_in(key, 11)
    noise_key = jax.random.fold_in(key, 0)
    return jnp.clip(jax.random.normal(noise_key, (CHAIN_LENGTH, CHAIN_LENGTH, CZ), jnp.float32), -4.0, 4.0).astype(jnp.bfloat16)


def draw_coupling_to_groups(key, part):
    columns = shared_columns(key)
    return (columns / 11.3).astype(jnp.bfloat16)


def with_ends(entries, key, smallest, top_value):
    longest = entries.shape.index(max(entries.shape))
    spots = []
    for shift in (0, 1):
        where = [jax.random.randint(jax.random.fold_in(key, axis), (), 0, length) for axis, length in enumerate(entries.shape)]
        where[longest] = (where[longest] + shift) % entries.shape[longest]
        spots.append(tuple(where))
    return entries.at[spots[0]].set(smallest).at[spots[1]].set(top_value)


def shard_levels(rng, extent, cuts, low, largest):
    def one(axis_at, shards_of):
        heights = jax.random.uniform(jax.random.fold_in(jax.random.fold_in(rng, 6), axis_at), (shards_of,), jnp.float32, low / len(cuts), largest / len(cuts))
        return jnp.repeat(jnp.exp(heights), extent[axis_at] // shards_of).reshape((-1,) + (1,) * (len(extent) - axis_at - 1))

    level = one(*cuts[0])
    for cut in cuts[1:]:
        level = level * one(*cut)
    return level


def scatter_about(rng, shape, width, limit, cuts=(), kind=jnp.bfloat16):
    values = width * jax.random.normal(rng, shape, jnp.float32)
    if cuts:
        values = values * shard_levels(rng, shape, cuts, -0.22, 0.18)
    return jnp.clip(values, -limit, limit).astype(kind)


def setup_inputs(seed: int = 0, part: int = 0) -> dict:
    arg_keys = jax.random.split(jax.random.key(seed), 11)
    part_keys = jax.random.split(jax.random.fold_in(arg_keys[10], part), 11)
    homolog_embedding = scatter_about(part_keys[0], (HOMOLOG_NUMBER, CHAIN_LENGTH, FEATURE_DEPTH), 1.0, 6.0, ((1, 16),))
    coupling_embedding = draw_coupling_embedding(jax.random.fold_in(jax.random.fold_in(arg_keys[10], part), 71), part)
    entry_indicator = with_ends((jax.random.randint(part_keys[2], (HOMOLOG_NUMBER, CHAIN_LENGTH), 0, 8) < 7).astype(jnp.int32), jax.random.fold_in(part_keys[2], 1), 0, 1)
    nonpadding_indicator = with_ends((jax.random.randint(part_keys[3], (CHAIN_LENGTH,), 0, 16) < 15).astype(jnp.int32), jax.random.fold_in(part_keys[3], 1), 0, 1)
    first_factor_matrix = scatter_about(arg_keys[4], (FEATURE_DEPTH, FACTOR_WIDE), FEATURE_DEPTH ** -0.5, 0.75)
    second_factor_matrix = scatter_about(arg_keys[5], (FEATURE_DEPTH, FACTOR_WIDE), FEATURE_DEPTH ** -0.5, 0.75)
    tensor_product_matrix = scatter_about(arg_keys[6], (FACTOR_WIDE * FACTOR_WIDE, CZ), (FACTOR_WIDE * FACTOR_WIDE // 64) ** -0.5, 1.5)
    coupling_to_groups = draw_coupling_to_groups(jax.random.fold_in(arg_keys[10], 71), part)
    query_key_gate_matrix = scatter_about(arg_keys[8], (FEATURE_DEPTH, 4 * ATTN_GROUPS * ATTN_DIM), FEATURE_DEPTH ** -0.5, 0.75)
    attention_final_matrix = scatter_about(arg_keys[9], (ATTN_GROUPS * ATTN_DIM, FEATURE_DEPTH), (ATTN_GROUPS * ATTN_DIM) ** -0.5, 0.375)
    return dict(homolog_embedding=homolog_embedding, coupling_embedding=coupling_embedding, entry_indicator=entry_indicator, nonpadding_indicator=nonpadding_indicator, first_factor_matrix=first_factor_matrix, second_factor_matrix=second_factor_matrix, tensor_product_matrix=tensor_product_matrix, coupling_to_groups=coupling_to_groups, query_key_gate_matrix=query_key_gate_matrix, attention_final_matrix=attention_final_matrix)


epsilon = 1e-05

def standardize_features(values):
    widened = values.astype(jnp.float32)
    average = lax.optimization_barrier(jnp.mean(widened, axis=-1, keepdims=True))
    centred = widened - average
    spread = lax.optimization_barrier(jnp.mean(centred * centred, axis=-1, keepdims=True))
    return centred * lax.rsqrt(spread + epsilon)

def reference(homolog_embedding, coupling_embedding, entry_indicator, nonpadding_indicator, first_factor_matrix, second_factor_matrix, tensor_product_matrix, coupling_to_groups, query_key_gate_matrix, attention_final_matrix):
    standardized_homologs = standardize_features(homolog_embedding).astype(jnp.bfloat16)
    active_flag = entry_indicator * nonpadding_indicator[None, :]
    active_float = active_flag.astype(jnp.float32)
    left_operand = (jnp.dot(standardized_homologs, first_factor_matrix, preferred_element_type=jnp.float32) * active_float[..., None]).astype(jnp.bfloat16)
    right_operand = (jnp.dot(standardized_homologs, second_factor_matrix, preferred_element_type=jnp.float32) * active_float[..., None]).astype(jnp.bfloat16)
    right_wide = right_operand.astype(jnp.float32)

    def opm_block(row_start):
        left_block = lax.dynamic_slice_in_dim(left_operand, row_start, TOK_DEV, 1).astype(jnp.float32)
        mask_block = lax.dynamic_slice_in_dim(active_float, row_start, TOK_DEV, 1)
        outer_prod = jnp.einsum('sic,sjd->ijcd', left_block, right_wide)
        pair_count = jnp.einsum('si,sj->ij', mask_block, active_float)
        averaged = (outer_prod / jnp.maximum(pair_count, 1.0)[..., None, None]).astype(jnp.bfloat16)
        averaged = averaged.reshape(TOK_DEV, CHAIN_LENGTH, FACTOR_WIDE * FACTOR_WIDE)
        return jnp.dot(averaged, tensor_product_matrix, preferred_element_type=jnp.float32)
    starts = jnp.arange(CHAIN_LENGTH // TOK_DEV, dtype=jnp.int32) * TOK_DEV
    update = lax.map(opm_block, starts).reshape(CHAIN_LENGTH, CHAIN_LENGTH, CZ)
    pair_output = (coupling_embedding.astype(jnp.float32) + update).astype(jnp.bfloat16)
    normed_pair = standardize_features(pair_output).astype(jnp.bfloat16)
    bias = jnp.dot(normed_pair, coupling_to_groups, preferred_element_type=jnp.float32).astype(jnp.bfloat16)
    bias_heads = jnp.transpose(bias, (2, 0, 1)).astype(jnp.float32)
    projected_values = jnp.dot(standardized_homologs, query_key_gate_matrix, preferred_element_type=jnp.float32).astype(jnp.bfloat16)
    scale = 1.0 / math.sqrt(ATTN_DIM)

    def attend(sequence):
        projected_row, key_mask = sequence
        blocks = projected_row.astype(jnp.float32).reshape(CHAIN_LENGTH, 4, ATTN_GROUPS, ATTN_DIM)
        logits = jnp.einsum('ihd,jhd->hij', blocks[:, 0], blocks[:, 1]) * scale + bias_heads
        logits = jnp.where(key_mask[None, None, :] > 0, logits, -1000000000.0)
        weights = jax.nn.softmax(logits, axis=-1).astype(jnp.bfloat16)
        attended = jnp.einsum('hij,jhd->ihd', weights.astype(jnp.float32), blocks[:, 2])
        gated = attended * jax.nn.sigmoid(blocks[:, 3])
        return gated.astype(jnp.bfloat16).reshape(CHAIN_LENGTH, ATTN_GROUPS * ATTN_DIM)
    gated_out = lax.map(attend, (projected_values, active_float))
    increment_term = jnp.dot(gated_out, attention_final_matrix, preferred_element_type=jnp.float32)
    refreshed_homologs = (homolog_embedding.astype(jnp.float32) + increment_term).astype(jnp.bfloat16)
    return (pair_output, refreshed_homologs)
```

```python
import functools
import math

import jax
import jax.numpy as jnp
from jax import lax
from jax.experimental import pallas as pl
from jax.experimental.pallas import tpu as pltpu
from jax.sharding import PartitionSpec as P

F32 = jnp.float32
BF16 = jnp.bfloat16
HEADS = 8
DIM = 32
FACTOR = 32
EPS = 1e-05
MESH = pl.DeviceIdType.MESH


def nn(a, b):
    return lax.dot_general(a, b, (((1,), (0,)), ((), ())), preferred_element_type=F32)


def nt(a, b):
    return lax.dot_general(a, b, (((1,), (1,)), ((), ())), preferred_element_type=F32)


def standardize(x):
    mean = jnp.mean(x, axis=-1, keepdims=True)
    centred = x - mean
    spread = jnp.mean(centred * centred, axis=-1, keepdims=True)
    return centred * lax.rsqrt(spread + EPS)


def iota(shape, dim):
    return lax.broadcasted_iota(jnp.int32, shape, dim)


def kernel(
    devices, seqs, own,
    h_ref, pair_ref, entry_ref, pad_ref, w1_ref, w2_ref, wt_ref, cg_ref, wq_ref, wo_ref,
    pair_out, out_ref,
    g_ref, n_ref, nf_ref, n2_ref, q_ref, a_ref, rs_ref, t_ref, lt_ref, live_ref, cap_ref,
    bias_ref, wf_ref, wp_ref, bd_ref, bv_ref,
    send_r, recv_r, send_l, recv_l, send_s, recv_s,
):
    half = seqs // 2
    rows = half * own
    length = devices * own
    ch = h_ref.shape[1]
    chips = devices // 2
    me = lax.axis_index("row")
    core = me % 2
    chip = me // 2
    odd = chip % 2
    pos = (1 - odd) * (chip // 2) + odd * (chips - 1 - chip // 2)

    def device_at(p):
        p = (p + chips) % chips
        hi = (2 * p) // chips
        c = (1 - hi) * 2 * p + hi * (2 * (chips - 1 - p) + 1)
        return 2 * c + core

    right, left, sibling = device_at(pos + 1), device_at(pos - 1), 2 * chip + 1 - core

    barrier = pltpu.get_barrier_semaphore()
    for other in (left, right, sibling):
        pl.semaphore_signal(barrier, inc=1, device_id={"row": other}, device_id_type=MESH)

    e0 = (iota((ch, 2 * ch), 0) == iota((ch, 2 * ch), 1)).astype(BF16)
    e1 = (iota((ch, 2 * ch), 0) + ch == iota((ch, 2 * ch), 1)).astype(BF16)
    piece = 256

    def prepare(k, _):
        at = pl.multiple_of(k * piece, piece)
        parts = []
        for hf in range(2):
            where = pl.ds(hf * rows + at, piece)
            normed = standardize(h_ref[where, :].astype(F32)).astype(BF16)
            n_ref[where, :] = normed
            nf_ref[where, :] = normed.astype(F32)
            parts.append(normed)
        g_ref[me, pl.ds(at, piece), :] = (nn(parts[0], e0) + nn(parts[1], e1)).astype(BF16)
        return 0

    lax.fori_loop(0, rows // piece, prepare, 0)
    diag = jnp.where(iota((own, own), 0) == iota((own, own), 1), pad_ref[...], 0).astype(F32).astype(BF16)
    live_own = nt(diag, entry_ref[...].astype(F32).astype(BF16))
    g_ref[me, rows : rows + 2 * own, :] = jnp.concatenate(
        [live_own[:, :half], live_own[:, half:]], axis=0
    ).astype(BF16)

    pl.semaphore_wait(barrier, 3)

    def move(origin, to, ssem, rsem):
        return pltpu.make_async_remote_copy(
            src_ref=g_ref.at[origin],
            dst_ref=g_ref.at[origin],
            send_sem=ssem,
            recv_sem=rsem,
            device_id={"row": to},
            device_id_type=MESH,
        )

    steps_r = chips // 2
    steps_l = chips - 1 - steps_r
    sent = []

    def send(origin, to, ssem, rsem):
        copy = move(origin, to, ssem, rsem)
        copy.start()
        sent.append(copy)

    send(me, right, send_r.at[0], recv_r.at[0])
    if steps_l:
        send(me, left, send_l.at[0], recv_l.at[0])
    send(me, sibling, send_s.at[0], recv_s.at[0])

    scale = 1.0 / math.sqrt(DIM)
    width = HEADS * DIM
    lanes = 2 * ch
    wk = wq_ref[:, width : 2 * width]
    wv = wq_ref[:, 2 * width : 3 * width]
    for hf, e in enumerate((e0, e1)):
        wkt = lax.dot_general(wk, e, (((0,), (0,)), ((), ())), preferred_element_type=F32)
        head = iota((width, lanes), 0) // DIM
        for hd in range(HEADS):
            bd_ref[hf, :, hd * lanes : (hd + 1) * lanes] = jnp.where(head == hd, wkt, 0.0).astype(BF16)
    zero = jnp.zeros((ch, width), F32)
    column = iota((lanes, width), 1) // DIM
    for hf in range(2):
        stacked = jnp.concatenate([wv.astype(F32), zero] if hf == 0 else [zero, wv.astype(F32)], axis=0)
        for hd in range(HEADS):
            bv_ref[hf, hd * lanes : (hd + 1) * lanes, :] = jnp.where(column == hd, stacked, 0.0).astype(BF16)
    wf_ref[...] = wt_ref[...].astype(F32)
    per = 128 // FACTOR
    for k in range(FACTOR // per):
        rowsets = [wf_ref[pl.ds(k * per + d, FACTOR, stride=FACTOR), :] for d in range(per)]
        wp_ref[:, k * 128 : (k + 1) * 128] = jnp.concatenate(rowsets, axis=0).T.astype(BF16)
    w2 = w2_ref[...]
    w2t = jnp.concatenate(
        [lax.dot_general(w2, e, (((0,), (0,)), ((), ())), preferred_element_type=F32) for e in (e0, e1)], axis=0
    ).astype(BF16)
    eye = (iota((own, HEADS), 0) == iota((own, HEADS), 1)).astype(BF16)
    cgt = nt(eye, cg_ref[...]).astype(BF16)
    w1 = w1_ref[...]
    for i in range(own):
        n_i = nf_ref[pl.ds(i, seqs, stride=own), :].astype(BF16)
        lt = lax.dot_general(w1, n_i, (((0,), (1,)), ((), ())), preferred_element_type=F32)
        lt_ref[i * FACTOR : (i + 1) * FACTOR, :] = (lt * live_own[i : i + 1, :]).astype(BF16)

    group = 256 // own

    def queries(k, _):
        at = pl.multiple_of(k * 256, 256)
        for hf in range(2):
            q = nn(n_ref[pl.ds(hf * rows + at, 256), :], wq_ref[:, :width]).astype(BF16)
            folded = nn(q, bd_ref[hf]) * scale
            for s in range(group):
                block = folded[s * own : (s + 1) * own]
                tall = jnp.concatenate([block[:, hd * lanes : (hd + 1) * lanes] for hd in range(HEADS)], axis=0)
                q_ref[k * group + s, hf * HEADS * own : (hf + 1) * HEADS * own, :] = tall.astype(BF16)
        return 0

    lax.fori_loop(0, rows // 256, queries, 0)

    for t in range(steps_r):
        origin = device_at(pos - 1 - t)
        move(origin, right, send_r.at[t], recv_r.at[t]).wait_recv()
        if t + 1 < steps_r:
            send(origin, right, send_r.at[t + 1], recv_r.at[t + 1])
        send(origin, sibling, send_s.at[1 + t], recv_s.at[1 + t])
        if t < steps_l:
            origin = device_at(pos + 1 + t)
            move(origin, left, send_l.at[t], recv_l.at[t]).wait_recv()
            if t + 1 < steps_l:
                send(origin, left, send_l.at[t + 1], recv_l.at[t + 1])
            send(origin, sibling, send_s.at[1 + steps_r + t], recv_s.at[1 + steps_r + t])
    for t in range(chips):
        origin = device_at(pos if t == 0 else (pos - t if t <= steps_r else pos + t - steps_r))
        origin = origin + 1 - 2 * core
        move(origin, sibling, send_s.at[t], recv_s.at[t]).wait_recv()
    for copy in sent:
        copy.wait_send()

    def relay(p, _):
        at = pl.ds(pl.multiple_of(p * 16, 16), 16)
        for c in range(chips):
            x = g_ref[2 * c, at, :].astype(F32)
            y = g_ref[2 * c + 1, at, :].astype(F32)
            n2_ref[2 * p, 16 * c : 16 * c + 16, :] = jnp.concatenate([x[:8], y[:8]], axis=0).astype(BF16)
            n2_ref[2 * p + 1, 16 * c : 16 * c + 16, :] = jnp.concatenate([x[8:], y[8:]], axis=0).astype(BF16)
        return 0

    lax.fori_loop(0, half // 2, relay, 0)

    live_b = live_own.astype(BF16)
    for jc in range(length // 128):
        js = slice(jc * 128, (jc + 1) * 128)
        masks = [g_ref[r, rows : rows + 2 * own, :].astype(F32) for r in range(jc * 16, (jc + 1) * 16)]
        for hf in range(2):
            tall = jnp.concatenate([m[hf * own : (hf + 1) * own] for m in masks], axis=0)
            live_ref[jc, hf * half : (hf + 1) * half, :] = tall.T
        live_j = live_ref[jc]
        cap_ref[jc] = jnp.where(live_j > 0, 3e38, -1000000000.0)
        inverse = 1.0 / jnp.maximum(nn(live_b, live_j.astype(BF16)), 1.0)

        def factor(s, _):
            block = nt(w2t, n2_ref[s, js, :])
            rs_ref[pl.ds(pl.multiple_of(s * 2 * FACTOR, 2 * FACTOR), 2 * FACTOR), :] = jnp.concatenate(
                [
                    block[:FACTOR] * live_ref[jc, pl.ds(s, 1), :],
                    block[FACTOR:] * live_ref[jc, pl.ds(half + s, 1), :],
                ],
                axis=0,
            )
            return 0

        lax.fori_loop(0, half, factor, 0, unroll=4)

        def outer(k, _):
            columns = []
            for d in range(2):
                columns.append(
                    jnp.concatenate(
                        [
                            rs_ref[pl.ds(hf * FACTOR + 2 * k + d, half, stride=2 * FACTOR), :].astype(BF16)
                            for hf in range(2)
                        ],
                        axis=0,
                    )
                )
            prod = nn(lt_ref[...], jnp.concatenate(columns, axis=1))
            for i in range(own):
                for d in range(2):
                    tile = prod[i * FACTOR : (i + 1) * FACTOR, d * 128 : (d + 1) * 128] * inverse[i : i + 1, :]
                    at = pl.multiple_of((2 * k + d) * FACTOR, FACTOR)
                    t_ref[i, pl.ds(at, FACTOR), :] = tile.astype(BF16)
            return 0

        lax.fori_loop(0, FACTOR // 2, outer, 0)

        for i in range(own):
            update = nn(wp_ref[...], t_ref[i]).T
            pair = (pair_ref[i, js, :].astype(F32) + update).astype(BF16)
            pair_out[i, js, :] = pair
            normed = standardize(pair.astype(F32)).astype(BF16)
            bias_ref[jc, pl.ds(i, HEADS, stride=own), :] = nt(cgt, normed).astype(BF16).astype(F32)

    def cap_row(s):
        return jnp.concatenate([cap_ref[jc, pl.ds(s, 1), :] for jc in range(length // 128)], axis=1)

    def attend(p, _):
        results = []
        for k in range(2):
            s = 2 * p + k
            keys = n2_ref[s]
            logits = nt(q_ref[s], keys)
            bias = jnp.concatenate([bias_ref[jc] for jc in range(length // 128)], axis=1)
            m = HEADS * own
            logits = jnp.concatenate(
                [
                    jnp.minimum(logits[:m] + bias, cap_row(s)),
                    jnp.minimum(logits[m:] + bias, cap_row(half + s)),
                ],
                axis=0,
            )
            top = jnp.max(logits, axis=1, keepdims=True)
            weights = jnp.exp(logits - top)
            total = jnp.sum(weights, axis=1, keepdims=True)
            results.append(nn(weights.astype(BF16), keys) * (1.0 / total))
        at = pl.ds(pl.multiple_of(p * 2 * own, 2 * own), 2 * own)
        for hf in range(2):
            for hd in range(HEADS):
                start = (hf * HEADS + hd) * own
                tile = jnp.concatenate([r[start : start + own] for r in results], axis=0)
                a_ref[hf, at, hd * lanes : (hd + 1) * lanes] = tile.astype(BF16)
        return 0

    lax.fori_loop(0, half // 2, attend, 0)

    def finish(k, _):
        at = pl.multiple_of(k * 256, 256)
        for hf in range(2):
            where = pl.ds(hf * rows + at, 256)
            attended = nn(a_ref[hf, pl.ds(at, 256), :], bv_ref[hf])
            gate = nn(n_ref[where, :], wq_ref[:, 3 * width :]).astype(BF16).astype(F32)
            gated = (attended * jax.nn.sigmoid(gate)).astype(BF16)
            increment = nn(gated, wo_ref[...])
            out_ref[where, :] = (h_ref[where, :].astype(F32) + increment).astype(BF16)
        return 0

    lax.fori_loop(0, rows // 256, finish, 0)


def on_device(devices, homolog, coupling, entry, nonpadding, w1, w2, wt, cg, wq, wo):
    seqs, own, ch = homolog.shape
    half = seqs // 2
    rows = half * own
    length = coupling.shape[1]
    chips = devices // 2
    lanes = 2 * ch
    dma = pltpu.SemaphoreType.DMA
    vmem = pl.BlockSpec(memory_space=pltpu.VMEM)
    pair_output, refreshed = pl.pallas_call(
        functools.partial(kernel, devices, seqs, own),
        out_shape=(
            jax.ShapeDtypeStruct(coupling.shape, BF16),
            jax.ShapeDtypeStruct((seqs * own, ch), BF16),
        ),
        in_specs=[vmem] * 10,
        out_specs=(vmem, vmem),
        scratch_shapes=[
            pltpu.VMEM((devices, rows + 2 * own, lanes), BF16),
            pltpu.VMEM((2 * rows, ch), BF16),
            pltpu.VMEM((2 * rows, ch), F32),
            pltpu.VMEM((half, length, lanes), BF16),
            pltpu.VMEM((half, 2 * HEADS * own, lanes), BF16),
            pltpu.VMEM((2, rows, HEADS * lanes), BF16),
            pltpu.VMEM((half * 2 * FACTOR, 128), F32),
            pltpu.VMEM((own, FACTOR * FACTOR, 128), BF16),
            pltpu.VMEM((own * FACTOR, seqs), BF16),
            pltpu.VMEM((length // 128, seqs, 128), F32),
            pltpu.VMEM((length // 128, seqs, 128), F32),
            pltpu.VMEM((length // 128, HEADS * own, 128), F32),
            pltpu.VMEM((FACTOR * FACTOR, 128), F32),
            pltpu.VMEM((128, FACTOR * FACTOR), BF16),
            pltpu.VMEM((2, HEADS * DIM, HEADS * lanes), BF16),
            pltpu.VMEM((2, HEADS * lanes, HEADS * DIM), BF16),
            dma((chips,)), dma((chips,)), dma((chips,)), dma((chips,)), dma((chips,)), dma((chips,)),
        ],
        compiler_params=pltpu.CompilerParams(
            collective_id=0, has_side_effects=True, vmem_limit_bytes=62 * 1024 * 1024
        ),
    )(
        homolog.reshape(seqs * own, ch), coupling, entry, nonpadding.reshape(1, own),
        w1, w2, wt, cg, wq, wo,
    )
    return pair_output, refreshed.reshape(seqs, own, ch)


def solution(mesh):
    return jax.shard_map(
        functools.partial(on_device, mesh.shape["row"]),
        mesh=mesh,
        in_specs=(
            P("groups", "row", None),
            P(("groups", "row"), None, None),
            P("groups", "row"),
            P(("groups", "row")),
            P(), P(), P(), P(), P(), P(),
        ),
        out_specs=(P(("groups", "row"), None, None), P("groups", "row", None)),
        check_vma=False,
    )
```

```python
import functools
import math

import jax
import jax.numpy as jnp
from jax import lax
from jax.experimental import pallas as pl
from jax.experimental.pallas import tpu as pltpu
from jax.sharding import PartitionSpec as P

F32 = jnp.float32
BF16 = jnp.bfloat16
HEADS = 8
DIM = 32
FACTOR = 32
EPS = 1e-05
PIECES = 4
MESH = pl.DeviceIdType.MESH


def nn(a, b):
    return lax.dot_general(a, b, (((1,), (0,)), ((), ())), preferred_element_type=F32)


def nt(a, b):
    return lax.dot_general(a, b, (((1,), (1,)), ((), ())), preferred_element_type=F32)


def standardize(x):
    mean = jnp.mean(x, axis=-1, keepdims=True)
    centred = x - mean
    spread = jnp.mean(centred * centred, axis=-1, keepdims=True)
    return centred * lax.rsqrt(spread + EPS)


def iota(shape, dim):
    return lax.broadcasted_iota(jnp.int32, shape, dim)


def kernel(
    devices, seqs, own,
    h_ref, pair_ref, entry_ref, pad_ref, w1_ref, w2_ref, wt_ref, cg_ref, wq_ref, wo_ref,
    pair_out, out_ref,
    g_ref, n_ref, nf_ref, n2_ref, n2t_ref, q_ref, a_ref, rs_ref, t_ref, lt_ref, live_ref, cap_ref,
    bias_ref, wf_ref, wp_ref, bd_ref, bv_ref,
    send_r, recv_r, send_l, recv_l, send_s, recv_s,
):
    half = seqs // 2
    rows = half * own
    length = devices * own
    ch = h_ref.shape[1]
    head = 2 * own
    flip = length == 128
    chips = devices // 2
    me = lax.axis_index("row")
    core = me % 2
    chip = me // 2
    odd = chip % 2
    pos = (1 - odd) * (chip // 2) + odd * (chips - 1 - chip // 2)

    def device_at(p):
        p = (p + chips) % chips
        hi = (2 * p) // chips
        c = (1 - hi) * 2 * p + hi * (2 * (chips - 1 - p) + 1)
        return 2 * c + core

    right, left, sibling = device_at(pos + 1), device_at(pos - 1), 2 * chip + 1 - core

    barrier = pltpu.get_barrier_semaphore()
    for other in (left, right, sibling):
        pl.semaphore_signal(barrier, inc=1, device_id={"row": other}, device_id_type=MESH)

    e0 = (iota((ch, 2 * ch), 0) == iota((ch, 2 * ch), 1)).astype(BF16)
    e1 = (iota((ch, 2 * ch), 0) + ch == iota((ch, 2 * ch), 1)).astype(BF16)
    piece = 256

    def prepare(k, _):
        at = pl.multiple_of(k * piece, piece)
        parts = []
        for hf in range(2):
            where = pl.ds(hf * rows + at, piece)
            normed = standardize(h_ref[where, :].astype(F32)).astype(BF16)
            n_ref[where, :] = normed
            nf_ref[where, :] = normed.astype(F32)
            parts.append(normed)
        g_ref[me, pl.ds(head + at, piece), :] = (nn(parts[0], e0) + nn(parts[1], e1)).astype(BF16)
        return 0

    lax.fori_loop(0, rows // piece, prepare, 0)
    diag = jnp.where(iota((own, own), 0) == iota((own, own), 1), pad_ref[...], 0).astype(F32).astype(BF16)
    live_own = nt(diag, entry_ref[...].astype(F32).astype(BF16))
    g_ref[me, :head, :] = jnp.concatenate(
        [live_own[:, :half], live_own[:, half:]], axis=0
    ).astype(BF16)

    pl.semaphore_wait(barrier, 3)

    hops = chips // 2
    size = rows // PIECES

    def move(origin, to, c, ssem, rsem):
        span = pl.ds(0, size + head) if c == 0 else pl.ds(head + c * size, size)
        return pltpu.make_async_remote_copy(
            src_ref=g_ref.at[origin, span],
            dst_ref=g_ref.at[origin, span],
            send_sem=ssem,
            recv_sem=rsem,
            device_id={"row": to},
            device_id_type=MESH,
        )

    sent = []

    def send(*what):
        copy = move(*what)
        copy.start()
        sent.append(copy)

    def reach(c):
        return hops - c % 2, hops - 1 + c % 2

    for c in range(PIECES):
        far_r, far_l = reach(c)
        if far_r:
            send(me, right, c, send_r.at[0, c], recv_r.at[0, c])
        if far_l:
            send(me, left, c, send_l.at[0, c], recv_l.at[0, c])
    for c in range(PIECES):
        send(me, sibling, c, send_s.at[0, c], recv_s.at[0, c])

    scale = 1.0 / math.sqrt(DIM)
    width = HEADS * DIM
    lanes = 2 * ch
    wk = wq_ref[:, width : 2 * width]
    wv = wq_ref[:, 2 * width : 3 * width]
    for hf, e in enumerate((e0, e1)):
        wkt = lax.dot_general(wk, e, (((0,), (0,)), ((), ())), preferred_element_type=F32)
        owner = iota((width, lanes), 0) // DIM
        for hd in range(HEADS):
            bd_ref[hf, :, hd * lanes : (hd + 1) * lanes] = jnp.where(owner == hd, wkt, 0.0).astype(BF16)
    zero = jnp.zeros((ch, width), F32)
    column = iota((lanes, width), 1) // DIM
    for hf in range(2):
        stacked = jnp.concatenate([wv.astype(F32), zero] if hf == 0 else [zero, wv.astype(F32)], axis=0)
        for hd in range(HEADS):
            bv_ref[hf, hd * lanes : (hd + 1) * lanes, :] = jnp.where(column == hd, stacked, 0.0).astype(BF16)
    wf_ref[...] = wt_ref[...].astype(F32)
    per = 128 // FACTOR
    for k in range(FACTOR // per):
        rowsets = [wf_ref[pl.ds(k * per + d, FACTOR, stride=FACTOR), :] for d in range(per)]
        wp_ref[:, k * 128 : (k + 1) * 128] = jnp.concatenate(rowsets, axis=0).T.astype(BF16)
    w2 = w2_ref[...]
    w2t = jnp.concatenate(
        [lax.dot_general(w2, e, (((0,), (0,)), ((), ())), preferred_element_type=F32) for e in (e0, e1)], axis=0
    ).astype(BF16)
    eye = (iota((own, HEADS), 0) == iota((own, HEADS), 1)).astype(BF16)
    cgt = nt(eye, cg_ref[...]).astype(BF16)
    w1 = w1_ref[...]
    for i in range(own):
        n_i = nf_ref[pl.ds(i, seqs, stride=own), :].astype(BF16)
        lt = lax.dot_general(w1, n_i, (((0,), (1,)), ((), ())), preferred_element_type=F32)
        lt_ref[i * FACTOR : (i + 1) * FACTOR, :] = (lt * live_own[i : i + 1, :]).astype(BF16)

    group = 256 // own

    def queries(k, _):
        at = pl.multiple_of(k * 256, 256)
        for hf in range(2):
            q = nn(n_ref[pl.ds(hf * rows + at, 256), :], wq_ref[:, :width]).astype(BF16)
            folded = nn(q, bd_ref[hf]) * scale
            for s in range(group):
                block = folded[s * own : (s + 1) * own]
                tall = jnp.concatenate([block[:, hd * lanes : (hd + 1) * lanes] for hd in range(HEADS)], axis=0)
                q_ref[k * group + s, hf * HEADS * own : (hf + 1) * HEADS * own, :] = tall.astype(BF16)
        return 0

    lax.fori_loop(0, rows // 256, queries, 0)

    def read_masks():
        for jc in range(length // 128):
            masks = [g_ref[r, :head, :].astype(F32) for r in range(jc * 16, (jc + 1) * 16)]
            for hf in range(2):
                tall = jnp.concatenate([m[hf * own : (hf + 1) * own] for m in masks], axis=0)
                live_ref[jc, hf * half : (hf + 1) * half, :] = tall.T

    def factor(s, block, jc):
        rs_ref[pl.ds(pl.multiple_of(s * 2 * FACTOR, 2 * FACTOR), 2 * FACTOR), :] = jnp.concatenate(
            [
                block[:FACTOR] * live_ref[jc, pl.ds(s, 1), :],
                block[FACTOR:] * live_ref[jc, pl.ds(half + s, 1), :],
            ],
            axis=0,
        )

    def relay(p, _):
        at = pl.ds(pl.multiple_of(head + p * 16, 16), 16)
        tiles = [g_ref[r, at, :].astype(F32) for r in range(devices)]
        for k in range(2):
            keys = jnp.concatenate([x[k * own : (k + 1) * own] for x in tiles], axis=0).astype(BF16)
            n2_ref[2 * p + k] = keys
            if flip:
                turned = keys.T
                n2t_ref[2 * p + k] = turned
                factor(2 * p + k, nn(w2t, turned), 0)
        return 0

    def work(c):
        far_r, far_l = reach(c)
        arrivals = [(pos, 0)] + [(pos - 1 - t, 1 + t) for t in range(far_r)]
        arrivals += [(pos + 1 + t, 1 + hops + t) for t in range(far_l)]
        for where, slot in arrivals:
            origin = device_at(where) + 1 - 2 * core
            move(origin, sibling, c, send_s.at[slot, c], recv_s.at[slot, c]).wait_recv()
        if c == 0:
            read_masks()
        pairs = half // 2 // PIECES
        lax.fori_loop(c * pairs, (c + 1) * pairs, relay, 0, unroll=2)

    for t in range(hops):
        ahead, back = device_at(pos - 1 - t), device_at(pos + 1 + t)
        for c in range(PIECES):
            far_r, far_l = reach(c)
            if t < far_r:
                move(ahead, right, c, send_r.at[t, c], recv_r.at[t, c]).wait_recv()
                if t + 1 < far_r:
                    send(ahead, right, c, send_r.at[t + 1, c], recv_r.at[t + 1, c])
                send(ahead, sibling, c, send_s.at[1 + t, c], recv_s.at[1 + t, c])
            if t < far_l:
                move(back, left, c, send_l.at[t, c], recv_l.at[t, c]).wait_recv()
                if t + 1 < far_l:
                    send(back, left, c, send_l.at[t + 1, c], recv_l.at[t + 1, c])
                send(back, sibling, c, send_s.at[1 + hops + t, c], recv_s.at[1 + hops + t, c])
            if t == hops - 1 and c > 0:
                work(c - 1)
    work(PIECES - 1)
    for copy in sent:
        copy.wait_send()

    live_b = live_own.astype(BF16)
    for jc in range(length // 128):
        js = slice(jc * 128, (jc + 1) * 128)
        live_j = live_ref[jc]
        cap_ref[jc] = jnp.where(live_j > 0, 3e38, -1000000000.0)
        inverse = 1.0 / jnp.maximum(nn(live_b, live_j.astype(BF16)), 1.0)

        if not flip:

            def late(s, _):
                factor(s, nt(w2t, n2_ref[s, js, :]), jc)
                return 0

            lax.fori_loop(0, half, late, 0, unroll=4)

        def outer(k, _):
            columns = []
            for d in range(2):
                columns.append(
                    jnp.concatenate(
                        [
                            rs_ref[pl.ds(hf * FACTOR + 2 * k + d, half, stride=2 * FACTOR), :].astype(BF16)
                            for hf in range(2)
                        ],
                        axis=0,
                    )
                )
            prod = nn(lt_ref[...], jnp.concatenate(columns, axis=1))
            for i in range(own):
                for d in range(2):
                    tile = prod[i * FACTOR : (i + 1) * FACTOR, d * 128 : (d + 1) * 128] * inverse[i : i + 1, :]
                    at = pl.multiple_of((2 * k + d) * FACTOR, FACTOR)
                    t_ref[i, pl.ds(at, FACTOR), :] = tile.astype(BF16)
            return 0

        lax.fori_loop(0, FACTOR // 2, outer, 0)

        for i in range(own):
            update = nn(wp_ref[...], t_ref[i]).T
            pair = (pair_ref[i, js, :].astype(F32) + update).astype(BF16)
            pair_out[i, js, :] = pair
            normed = standardize(pair.astype(F32)).astype(BF16)
            bias_ref[jc, pl.ds(i, HEADS, stride=own), :] = nt(cgt, normed).astype(BF16).astype(F32)

    def cap_row(s):
        return jnp.concatenate([cap_ref[jc, pl.ds(s, 1), :] for jc in range(length // 128)], axis=1)

    ones = jnp.ones((length, lanes), BF16)

    def attend(p, _):
        results = []
        for k in range(2):
            s = 2 * p + k
            keys = n2_ref[s]
            logits = nn(q_ref[s], n2t_ref[s]) if flip else nt(q_ref[s], keys)
            bias = jnp.concatenate([bias_ref[jc] for jc in range(length // 128)], axis=1)
            m = HEADS * own
            logits = jnp.concatenate(
                [
                    jnp.minimum(logits[:m] + bias, cap_row(s)),
                    jnp.minimum(logits[m:] + bias, cap_row(half + s)),
                ],
                axis=0,
            )
            top = jnp.max(logits, axis=1, keepdims=True)
            weights = jnp.exp(logits - top)
            mixed = nn(weights.astype(BF16), jnp.concatenate([keys, ones], axis=1))
            results.append(mixed[:, :lanes] / mixed[:, lanes:])
        at = pl.ds(pl.multiple_of(p * 2 * own, 2 * own), 2 * own)
        for hf in range(2):
            for hd in range(HEADS):
                start = (hf * HEADS + hd) * own
                tile = jnp.concatenate([r[start : start + own] for r in results], axis=0)
                a_ref[hf, at, hd * lanes : (hd + 1) * lanes] = tile.astype(BF16)
        return 0

    lax.fori_loop(0, half // 2, attend, 0, unroll=4 if flip else 1)

    def finish(k, _):
        at = pl.multiple_of(k * 256, 256)
        for hf in range(2):
            where = pl.ds(hf * rows + at, 256)
            attended = nn(a_ref[hf, pl.ds(at, 256), :], bv_ref[hf])
            gate = nn(n_ref[where, :], wq_ref[:, 3 * width :]).astype(BF16).astype(F32)
            gated = (attended * jax.nn.sigmoid(gate)).astype(BF16)
            increment = nn(gated, wo_ref[...])
            out_ref[where, :] = (h_ref[where, :].astype(F32) + increment).astype(BF16)
        return 0

    lax.fori_loop(0, rows // 256, finish, 0)


def on_device(devices, homolog, coupling, entry, nonpadding, w1, w2, wt, cg, wq, wo):
    seqs, own, ch = homolog.shape
    half = seqs // 2
    rows = half * own
    length = coupling.shape[1]
    chips = devices // 2
    lanes = 2 * ch
    dma = pltpu.SemaphoreType.DMA
    vmem = pl.BlockSpec(memory_space=pltpu.VMEM)
    pair_output, refreshed = pl.pallas_call(
        functools.partial(kernel, devices, seqs, own),
        out_shape=(
            jax.ShapeDtypeStruct(coupling.shape, BF16),
            jax.ShapeDtypeStruct((seqs * own, ch), BF16),
        ),
        in_specs=[vmem] * 10,
        out_specs=(vmem, vmem),
        scratch_shapes=[
            pltpu.VMEM((devices, rows + 2 * own, lanes), BF16),
            pltpu.VMEM((2 * rows, ch), BF16),
            pltpu.VMEM((2 * rows, ch), F32),
            pltpu.VMEM((half, length, lanes), BF16),
            pltpu.VMEM((half if length == 128 else 1, lanes, 128), BF16),
            pltpu.VMEM((half, 2 * HEADS * own, lanes), BF16),
            pltpu.VMEM((2, rows, HEADS * lanes), BF16),
            pltpu.VMEM((half * 2 * FACTOR, 128), F32),
            pltpu.VMEM((own, FACTOR * FACTOR, 128), BF16),
            pltpu.VMEM((own * FACTOR, seqs), BF16),
            pltpu.VMEM((length // 128, seqs, 128), F32),
            pltpu.VMEM((length // 128, seqs, 128), F32),
            pltpu.VMEM((length // 128, HEADS * own, 128), F32),
            pltpu.VMEM((FACTOR * FACTOR, 128), F32),
            pltpu.VMEM((128, FACTOR * FACTOR), BF16),
            pltpu.VMEM((2, HEADS * DIM, HEADS * lanes), BF16),
            pltpu.VMEM((2, HEADS * lanes, HEADS * DIM), BF16),
            dma((chips, PIECES)), dma((chips, PIECES)), dma((chips, PIECES)), dma((chips, PIECES)),
            dma((chips + 1, PIECES)), dma((chips + 1, PIECES)),
        ],
        compiler_params=pltpu.CompilerParams(
            collective_id=0, has_side_effects=True, vmem_limit_bytes=62 * 1024 * 1024
        ),
    )(
        homolog.reshape(seqs * own, ch), coupling, entry, nonpadding.reshape(1, own),
        w1, w2, wt, cg, wq, wo,
    )
    return pair_output, refreshed.reshape(seqs, own, ch)


def solution(mesh):
    return jax.shard_map(
        functools.partial(on_device, mesh.shape["row"]),
        mesh=mesh,
        in_specs=(
            P("groups", "row", None),
            P(("groups", "row"), None, None),
            P("groups", "row"),
            P(("groups", "row")),
            P(), P(), P(), P(), P(), P(),
        ),
        out_specs=(P(("groups", "row"), None, None), P("groups", "row", None)),
        check_vma=False,
    )
```

```python
import functools
import math

import jax
import jax.numpy as jnp
from jax import lax
from jax.experimental import pallas as pl
from jax.experimental.pallas import tpu as pltpu
from jax.sharding import PartitionSpec as P

F32 = jnp.float32
BF16 = jnp.bfloat16
HEADS = 8
DIM = 32
FACTOR = 32
EPS = 1e-05
PIECES = 4
MESH = pl.DeviceIdType.MESH


def nn(a, b):
    return lax.dot_general(a, b, (((1,), (0,)), ((), ())), preferred_element_type=F32)


def nt(a, b):
    return lax.dot_general(a, b, (((1,), (1,)), ((), ())), preferred_element_type=F32)


def standardize(x):
    mean = jnp.mean(x, axis=-1, keepdims=True)
    centred = x - mean
    spread = jnp.mean(centred * centred, axis=-1, keepdims=True)
    return centred * lax.rsqrt(spread + EPS)


def iota(shape, dim):
    return lax.broadcasted_iota(jnp.int32, shape, dim)


def kernel(
    devices, seqs, own,
    h_ref, pair_ref, entry_ref, pad_ref, w1_ref, w2_ref, wt_ref, cg_ref, wq_ref, wo_ref,
    pair_out, out_ref,
    g_ref, n_ref, nf_ref, n2_ref, n2t_ref, q_ref, a_ref, rs_ref, t_ref, lt_ref, live_ref, cap_ref,
    bias_ref, wf_ref, wp_ref, bd_ref, bv_ref,
    send_r, recv_r, send_l, recv_l, send_s, recv_s,
):
    half = seqs // 2
    rows = half * own
    length = devices * own
    ch = h_ref.shape[1]
    head = 2 * own
    flip = length == 128
    chips = devices // 2
    me = lax.axis_index("row")
    core = me % 2
    chip = me // 2
    odd = chip % 2
    pos = (1 - odd) * (chip // 2) + odd * (chips - 1 - chip // 2)

    def device_at(p):
        p = (p + chips) % chips
        hi = (2 * p) // chips
        c = (1 - hi) * 2 * p + hi * (2 * (chips - 1 - p) + 1)
        return 2 * c + core

    right, left, sibling = device_at(pos + 1), device_at(pos - 1), 2 * chip + 1 - core

    barrier = pltpu.get_barrier_semaphore()
    for other in (left, right, sibling):
        pl.semaphore_signal(barrier, inc=1, device_id={"row": other}, device_id_type=MESH)

    e0 = (iota((ch, 2 * ch), 0) == iota((ch, 2 * ch), 1)).astype(BF16)
    e1 = (iota((ch, 2 * ch), 0) + ch == iota((ch, 2 * ch), 1)).astype(BF16)
    piece = 256

    def prepare(k, _):
        at = pl.multiple_of(k * piece, piece)
        parts = []
        for hf in range(2):
            where = pl.ds(hf * rows + at, piece)
            normed = standardize(h_ref[where, :].astype(F32)).astype(BF16)
            n_ref[where, :] = normed
            nf_ref[where, :] = normed.astype(F32)
            parts.append(normed)
        g_ref[me, pl.ds(head + at, piece), :] = (nn(parts[0], e0) + nn(parts[1], e1)).astype(BF16)
        return 0

    lax.fori_loop(0, rows // piece, prepare, 0)
    diag = jnp.where(iota((own, own), 0) == iota((own, own), 1), pad_ref[...], 0).astype(F32).astype(BF16)
    live_own = nn(diag, entry_ref[...].astype(F32).astype(BF16))
    g_ref[me, :head, :] = jnp.concatenate(
        [live_own[:, :half], live_own[:, half:]], axis=0
    ).astype(BF16)

    pl.semaphore_wait(barrier, 3)

    hops = chips // 2
    size = rows // PIECES

    def move(origin, to, c, ssem, rsem):
        span = pl.ds(0, size + head) if c == 0 else pl.ds(head + c * size, size)
        return pltpu.make_async_remote_copy(
            src_ref=g_ref.at[origin, span],
            dst_ref=g_ref.at[origin, span],
            send_sem=ssem,
            recv_sem=rsem,
            device_id={"row": to},
            device_id_type=MESH,
        )

    sent = []

    def send(*what):
        copy = move(*what)
        copy.start()
        sent.append(copy)

    def reach(c):
        return hops - c % 2, hops - 1 + c % 2

    for c in range(PIECES):
        far_r, far_l = reach(c)
        if far_r:
            send(me, right, c, send_r.at[0, c], recv_r.at[0, c])
        if far_l:
            send(me, left, c, send_l.at[0, c], recv_l.at[0, c])
    for c in range(PIECES):
        send(me, sibling, c, send_s.at[0, c], recv_s.at[0, c])

    scale = 1.0 / math.sqrt(DIM)
    width = HEADS * DIM
    lanes = 2 * ch
    wk = wq_ref[:, width : 2 * width]
    wv = wq_ref[:, 2 * width : 3 * width]
    for hf, e in enumerate((e0, e1)):
        wkt = lax.dot_general(wk, e, (((0,), (0,)), ((), ())), preferred_element_type=F32)
        owner = iota((width, lanes), 0) // DIM
        for hd in range(HEADS):
            bd_ref[hf, :, hd * lanes : (hd + 1) * lanes] = jnp.where(owner == hd, wkt, 0.0).astype(BF16)
    zero = jnp.zeros((ch, width), F32)
    column = iota((lanes, width), 1) // DIM
    for hf in range(2):
        stacked = jnp.concatenate([wv.astype(F32), zero] if hf == 0 else [zero, wv.astype(F32)], axis=0)
        for hd in range(HEADS):
            bv_ref[hf, hd * lanes : (hd + 1) * lanes, :] = jnp.where(column == hd, stacked, 0.0).astype(BF16)
    wf_ref[...] = wt_ref[...].astype(F32)
    per = 128 // FACTOR
    for k in range(FACTOR // per):
        rowsets = [wf_ref[pl.ds(k * per + d, FACTOR, stride=FACTOR), :] for d in range(per)]
        wp_ref[:, k * 128 : (k + 1) * 128] = jnp.concatenate(rowsets, axis=0).T.astype(BF16)
    w2 = w2_ref[...]
    w2t = jnp.concatenate(
        [nn(w2, e) for e in (e0, e1)], axis=0
    ).astype(BF16)
    cgt = cg_ref[...]
    w1 = w1_ref[...]
    for i in range(own):
        n_i = nf_ref[pl.ds(i, seqs, stride=own), :].astype(BF16)
        lt = nt(w1, n_i)
        lt_ref[i * FACTOR : (i + 1) * FACTOR, :] = (lt * live_own[i : i + 1, :]).astype(BF16)

    group = 256 // own

    def queries(k, _):
        at = pl.multiple_of(k * 256, 256)
        for hf in range(2):
            q = nn(n_ref[pl.ds(hf * rows + at, 256), :], wq_ref[:, :width]).astype(BF16)
            folded = nn(q, bd_ref[hf]) * scale
            for s in range(group):
                block = folded[s * own : (s + 1) * own]
                tall = jnp.concatenate([block[:, hd * lanes : (hd + 1) * lanes] for hd in range(HEADS)], axis=0)
                q_ref[k * group + s, hf * HEADS * own : (hf + 1) * HEADS * own, :] = tall.astype(BF16)
        return 0

    lax.fori_loop(0, rows // 256, queries, 0)

    def read_masks():
        for jc in range(length // 128):
            masks = [g_ref[r, :head, :].astype(F32) for r in range(jc * 16, (jc + 1) * 16)]
            for hf in range(2):
                tall = jnp.concatenate([m[hf * own : (hf + 1) * own] for m in masks], axis=0)
                live_ref[jc, hf * half : (hf + 1) * half, :] = tall.T

    def factor(s, block, jc):
        rs_ref[pl.ds(pl.multiple_of(s * 2 * FACTOR, 2 * FACTOR), 2 * FACTOR), :] = jnp.concatenate(
            [
                block[:FACTOR] * live_ref[jc, pl.ds(s, 1), :],
                block[FACTOR:] * live_ref[jc, pl.ds(half + s, 1), :],
            ],
            axis=0,
        )

    def relay(p, _):
        at = pl.ds(pl.multiple_of(head + p * 16, 16), 16)
        tiles = [g_ref[r, at, :].astype(F32) for r in range(devices)]
        for k in range(2):
            keys = jnp.concatenate([x[k * own : (k + 1) * own] for x in tiles], axis=0).astype(BF16)
            n2_ref[2 * p + k] = keys
            if flip:
                turned = keys.T
                n2t_ref[2 * p + k] = turned
                factor(2 * p + k, nn(w2t, turned), 0)
        return 0

    def work(c):
        far_r, far_l = reach(c)
        arrivals = [(pos, 0)] + [(pos - 1 - t, 1 + t) for t in range(far_r)]
        arrivals += [(pos + 1 + t, 1 + hops + t) for t in range(far_l)]
        for where, slot in arrivals:
            origin = device_at(where) + 1 - 2 * core
            move(origin, sibling, c, send_s.at[slot, c], recv_s.at[slot, c]).wait_recv()
        if c == 0:
            read_masks()
        pairs = half // 2 // PIECES
        lax.fori_loop(c * pairs, (c + 1) * pairs, relay, 0, unroll=2)

    for t in range(hops):
        ahead, back = device_at(pos - 1 - t), device_at(pos + 1 + t)
        for c in range(PIECES):
            far_r, far_l = reach(c)
            if t < far_r:
                move(ahead, right, c, send_r.at[t, c], recv_r.at[t, c]).wait_recv()
                if t + 1 < far_r:
                    send(ahead, right, c, send_r.at[t + 1, c], recv_r.at[t + 1, c])
                send(ahead, sibling, c, send_s.at[1 + t, c], recv_s.at[1 + t, c])
            if t < far_l:
                move(back, left, c, send_l.at[t, c], recv_l.at[t, c]).wait_recv()
                if t + 1 < far_l:
                    send(back, left, c, send_l.at[t + 1, c], recv_l.at[t + 1, c])
                send(back, sibling, c, send_s.at[1 + hops + t, c], recv_s.at[1 + hops + t, c])
            if t == hops - 1 and c > 0:
                work(c - 1)
    work(PIECES - 1)
    for copy in sent:
        copy.wait_send()

    live_b = live_own.astype(BF16)
    for jc in range(length // 128):
        js = slice(jc * 128, (jc + 1) * 128)
        live_j = live_ref[jc]
        cap_ref[jc] = jnp.where(live_j > 0, 3e38, -1000000000.0)
        inverse = 1.0 / jnp.maximum(nn(live_b, live_j.astype(BF16)), 1.0)

        if not flip:

            def late(s, _):
                factor(s, nt(w2t, n2_ref[s, js, :]), jc)
                return 0

            lax.fori_loop(0, half, late, 0, unroll=4)

        def outer(k, _):
            columns = []
            for d in range(2):
                columns.append(
                    jnp.concatenate(
                        [
                            rs_ref[pl.ds(hf * FACTOR + 2 * k + d, half, stride=2 * FACTOR), :].astype(BF16)
                            for hf in range(2)
                        ],
                        axis=0,
                    )
                )
            prod = nn(lt_ref[...], jnp.concatenate(columns, axis=1))
            for i in range(own):
                for d in range(2):
                    tile = prod[i * FACTOR : (i + 1) * FACTOR, d * 128 : (d + 1) * 128] * inverse[i : i + 1, :]
                    at = pl.multiple_of((2 * k + d) * FACTOR, FACTOR)
                    t_ref[i, pl.ds(at, FACTOR), :] = tile.astype(BF16)
            return 0

        lax.fori_loop(0, FACTOR // 2, outer, 0)

        for i in range(own):
            update = nn(wp_ref[...], t_ref[i]).T
            pair = (pair_ref[i, js, :].astype(F32) + update).astype(BF16)
            pair_out[i, js, :] = pair
            normed = standardize(pair.astype(F32)).astype(BF16)
            bias_ref[jc, pl.ds(i, HEADS, stride=own), :] = nt(cgt, normed).astype(BF16).astype(F32)

    def cap_row(s):
        return jnp.concatenate([cap_ref[jc, pl.ds(s, 1), :] for jc in range(length // 128)], axis=1)

    ones = jnp.ones((length, lanes), BF16)

    def attend(p, _):
        results = []
        for k in range(2):
            s = 2 * p + k
            keys = n2_ref[s]
            logits = nn(q_ref[s], n2t_ref[s]) if flip else nt(q_ref[s], keys)
            bias = jnp.concatenate([bias_ref[jc] for jc in range(length // 128)], axis=1)
            m = HEADS * own
            logits = jnp.concatenate(
                [
                    jnp.minimum(logits[:m] + bias, cap_row(s)),
                    jnp.minimum(logits[m:] + bias, cap_row(half + s)),
                ],
                axis=0,
            )
            top = jnp.max(logits, axis=1, keepdims=True)
            weights = jnp.exp(logits - top)
            mixed = nn(weights.astype(BF16), jnp.concatenate([keys, ones], axis=1))
            results.append(mixed[:, :lanes] / mixed[:, lanes:])
        at = pl.ds(pl.multiple_of(p * 2 * own, 2 * own), 2 * own)
        for hf in range(2):
            for hd in range(HEADS):
                start = (hf * HEADS + hd) * own
                tile = jnp.concatenate([r[start : start + own] for r in results], axis=0)
                a_ref[hf, at, hd * lanes : (hd + 1) * lanes] = tile.astype(BF16)
        return 0

    lax.fori_loop(0, half // 2, attend, 0, unroll=8 if flip else 1)

    def finish(k, _):
        at = pl.multiple_of(k * 256, 256)
        for hf in range(2):
            where = pl.ds(hf * rows + at, 256)
            attended = nn(a_ref[hf, pl.ds(at, 256), :], bv_ref[hf])
            gate = nn(n_ref[where, :], wq_ref[:, 3 * width :]).astype(BF16).astype(F32)
            gated = (attended * jax.nn.sigmoid(gate)).astype(BF16)
            increment = nt(gated, wo_ref[...])
            out_ref[where, :] = (h_ref[where, :].astype(F32) + increment).astype(BF16)
        return 0

    lax.fori_loop(0, rows // 256, finish, 0)


def on_device(devices, homolog, coupling, entry, nonpadding, w1, w2, wt, cg, wq, wo):
    seqs, own, ch = homolog.shape
    half = seqs // 2
    rows = half * own
    length = coupling.shape[1]
    chips = devices // 2
    lanes = 2 * ch
    dma = pltpu.SemaphoreType.DMA
    vmem = pl.BlockSpec(memory_space=pltpu.VMEM)
    pair_output, refreshed = pl.pallas_call(
        functools.partial(kernel, devices, seqs, own),
        out_shape=(
            jax.ShapeDtypeStruct(coupling.shape, BF16),
            jax.ShapeDtypeStruct((seqs * own, ch), BF16),
        ),
        in_specs=[vmem] * 10,
        out_specs=(vmem, vmem),
        scratch_shapes=[
            pltpu.VMEM((devices, rows + 2 * own, lanes), BF16),
            pltpu.VMEM((2 * rows, ch), BF16),
            pltpu.VMEM((2 * rows, ch), F32),
            pltpu.VMEM((half, length, lanes), BF16),
            pltpu.VMEM((half if length == 128 else 1, lanes, 128), BF16),
            pltpu.VMEM((half, 2 * HEADS * own, lanes), BF16),
            pltpu.VMEM((2, rows, HEADS * lanes), BF16),
            pltpu.VMEM((half * 2 * FACTOR, 128), F32),
            pltpu.VMEM((own, FACTOR * FACTOR, 128), BF16),
            pltpu.VMEM((own * FACTOR, seqs), BF16),
            pltpu.VMEM((length // 128, seqs, 128), F32),
            pltpu.VMEM((length // 128, seqs, 128), F32),
            pltpu.VMEM((length // 128, HEADS * own, 128), F32),
            pltpu.VMEM((FACTOR * FACTOR, 128), F32),
            pltpu.VMEM((128, FACTOR * FACTOR), BF16),
            pltpu.VMEM((2, HEADS * DIM, HEADS * lanes), BF16),
            pltpu.VMEM((2, HEADS * lanes, HEADS * DIM), BF16),
            dma((chips, PIECES)), dma((chips, PIECES)), dma((chips, PIECES)), dma((chips, PIECES)),
            dma((chips + 1, PIECES)), dma((chips + 1, PIECES)),
        ],
        compiler_params=pltpu.CompilerParams(
            collective_id=0, has_side_effects=True, vmem_limit_bytes=62 * 1024 * 1024
        ),
    )(
        homolog.reshape(seqs * own, ch), coupling, entry.T, nonpadding.reshape(1, own),
        w1.T, w2.T, wt, cg.T, wq, wo.T,
    )
    return pair_output, refreshed.reshape(seqs, own, ch)


def solution(mesh):
    return jax.shard_map(
        functools.partial(on_device, mesh.shape["row"]),
        mesh=mesh,
        in_specs=(
            P("groups", "row", None),
            P(("groups", "row"), None, None),
            P("groups", "row"),
            P(("groups", "row")),
            P(), P(), P(), P(), P(), P(),
        ),
        out_specs=(P(("groups", "row"), None, None), P("groups", "row", None)),
        check_vma=False,
    )
```
